512 devices in a mesh: dom: 128 (over y, z, core), edge: 4 (over x).
Axes of the slice: x: 4, y: 8, z: 8, core: 2. Of those that a mesh axis runs over, the one named last changes fastest.
Arguments:
- node_feat: bfloat16 [32768, 512], P('dom'), may hold values from -6 to 6
- edge_feat: bfloat16 [262144, 512], P(('dom', 'edge')), may hold values from -6 to 6
- edge_slot: int32 [262144], P(('dom', 'edge')), may hold values from 0 to 2303, as said below
- edge_recv: int32 [262144], P(('dom', 'edge')), may hold values from 0 to 255
- send_list: int32 [128, 128, 16], P('dom'), may hold values from 0 to 255
- edge_w_edge: bfloat16 [512, 512], P('edge'), may hold values from -0.15625 to 0.15625
- edge_w_send: bfloat16 [512, 512], P('edge'), may hold values from -0.15625 to 0.15625
- edge_w_recv: bfloat16 [512, 512], P('edge'), may hold values from -0.15625 to 0.15625
- edge_w_out: bfloat16 [512, 512], P('edge'), may hold values from -0.25 to 0.25
- edge_gain: float32 [512], replicated, may hold values from 0.5 to 1.5
- node_w_self: bfloat16 [512, 512], P('edge'), may hold values from -0.1875 to 0.1875
- node_w_agg: bfloat16 [512, 512], P('edge'), may hold values from -0.1875 to 0.1875
- node_w_out: bfloat16 [512, 512], P('edge'), may hold values from -0.25 to 0.25
- node_gain: float32 [512], replicated, may hold values from 0.5 to 1.5
Outputs:
- node_out: bfloat16 [32768, 512], P('dom')
- edge_out: bfloat16 [262144, 512], P(('dom', 'edge'))
The draws below stay inside these ranges and needn't reach their ends.
Inputs may be any that keep to these rules, and one draw needn't show every extreme that they name: `edge_slot`: A value v >= 256 of an edge of partition p names a slot u % 16 of the list of partition u // 16 for p, with u = v - 256; that partition is never p.
All inputs are finite; a program needn't handle non-finite values.
Results may differ from the reference program's by a relative error of at most 0.018.
Values may be sent and summed in bfloat16 or wider, within the bound.
No kernel may reach another device: no remote copies, remote signals or barrier semaphores. Data moves between devices by JAX's collectives and lax.ppermute only.
A program may use at most 64 MiB of HBM per device.

```python
import jax
import jax.numpy as jnp
from jax import lax

D = 512
HID = 512
NODE_DEV = 256
SLOT = 16
EDGE_DEV = 512
NODES = 32768
EDGES = 262144
N_DOM = 128
N_EDGE = 4


def draw_edge_slot(key, part):
    key = jax.random.fold_in(key, 11)
    per_part = EDGE_DEV * N_EDGE

    def one_partition(part_key, owner):
        key_count, key_peer, key_place, key_coin, key_local, key_order = jax.random.split(part_key, 6)
        peer_index = jnp.arange(N_DOM, dtype=jnp.int32)
        distance = (peer_index - owner) % N_DOM
        counts = jax.random.randint(key_count, (N_DOM,), 1, SLOT + 1)
        nearby = (distance == 1) | (distance == 2) | (distance == N_DOM - 1) | (distance == N_DOM - 2)
        counts = jnp.where(nearby, SLOT, counts)
        counts = jnp.where(distance == 0, 0, counts)
        position = jnp.arange(per_part, dtype=jnp.int32)
        first_peer = jnp.minimum(position // SLOT, N_DOM - 1)
        first_live = (position < N_DOM * SLOT) & (position % SLOT < counts[first_peer])
        other_peer = jax.random.randint(key_peer, (per_part,), 0, N_DOM)
        other_place = jax.random.randint(key_place, (per_part,), 0, SLOT)
        other_live = other_place < counts[other_peer]
        coin = jax.random.randint(key_coin, (per_part,), 0, 2) == 1
        local_row = jax.random.randint(key_local, (per_part,), 0, NODE_DEV)
        chosen = jnp.where(coin & other_live, NODE_DEV + other_peer * SLOT + other_place, local_row)
        chosen = jnp.where(first_live, NODE_DEV + position, chosen)
        order = jax.random.permutation(key_order, per_part)
        return chosen[order]
    part_keys = jax.random.split(key, N_DOM)
    result = jax.vmap(one_partition)(part_keys, jnp.arange(N_DOM, dtype=jnp.int32))
    return result.reshape(-1).astype(jnp.int32)


def with_ends(values, key, least, top_value):
    longest = values.shape.index(max(values.shape))
    spots = []
    for shift in (0, 1):
        where = [jax.random.randint(jax.random.fold_in(key, axis), (), 0, length) for axis, length in enumerate(values.shape)]
        where[longest] = (where[longest] + shift) % values.shape[longest]
        spots.append(tuple(where))
    return values.at[spots[0]].set(least).at[spots[1]].set(top_value)


def level_of(rng, dims, pieces, low, largest):
    def one(dim, parts):
        steps = jax.random.uniform(jax.random.fold_in(jax.random.fold_in(rng, 6), dim), (parts,), jnp.float32, low / len(pieces), largest / len(pieces))
        return jnp.repeat(jnp.exp(steps), dims[dim] // parts).reshape((-1,) + (1,) * (len(dims) - dim - 1))

    loudness = one(*pieces[0])
    for cut in pieces[1:]:
        loudness = loudness * one(*cut)
    return loudness


def scatter_about(own_key, extent, scale, bound, cuts=(), kind=jnp.bfloat16):
    entries = scale * jax.random.normal(own_key, extent, jnp.float32)
    if cuts:
        entries = entries * level_of(own_key, extent, cuts, -0.22, 0.18)
    return jnp.clip(entries, -bound, bound).astype(kind)


def setup_inputs(seed: int = 0) -> dict:
    seeds = jax.random.split(jax.random.key(seed), 15)
    node_feat = scatter_about(seeds[0], (NODES, D), 1.0, 6.0, ((0, 128),))
    edge_feat = scatter_about(seeds[1], (EDGES, D), 1.0, 6.0, ((0, 512),))
    edge_slot = draw_edge_slot(jax.random.fold_in(seeds[14], 71), 0)
    edge_recv = with_ends(jax.random.randint(seeds[3], (EDGES,), 0, NODE_DEV), jax.random.fold_in(seeds[3], 1), 0, NODE_DEV - 1).astype(jnp.int32)
    send_list = with_ends(jax.random.randint(seeds[4], (N_DOM, N_DOM, SLOT), 0, NODE_DEV), jax.random.fold_in(seeds[4], 1), 0, NODE_DEV - 1).astype(jnp.int32)
    edge_w_edge = scatter_about(seeds[5], (D, HID), (3 * D) ** -0.5, 0.15625, ((0, 4),))
    edge_w_send = scatter_about(seeds[6], (D, HID), (3 * D) ** -0.5, 0.15625, ((0, 4),))
    edge_w_recv = scatter_about(seeds[7], (D, HID), (3 * D) ** -0.5, 0.15625, ((0, 4),))
    edge_w_out = scatter_about(seeds[8], (HID, D), HID ** -0.5, 0.25, ((0, 4),))
    edge_gain = jnp.clip(1.0 + 0.1 * jax.random.normal(seeds[9], (D,), jnp.float32), 0.5, 1.5)
    node_w_self = scatter_about(seeds[10], (D, HID), (2 * D) ** -0.5, 0.1875, ((0, 4),))
    node_w_agg = scatter_about(seeds[11], (D, HID), (2 * D) ** -0.5, 0.1875, ((0, 4),))
    node_w_out = scatter_about(seeds[12], (HID, D), HID ** -0.5, 0.25, ((0, 4),))
    node_gain = jnp.clip(1.0 + 0.1 * jax.random.normal(seeds[13], (D,), jnp.float32), 0.5, 1.5)
    return {"node_feat": node_feat, "edge_feat": edge_feat, "edge_slot": edge_slot, "edge_recv": edge_recv, "send_list": send_list, "edge_w_edge": edge_w_edge, "edge_w_send": edge_w_send, "edge_w_recv": edge_w_recv, "edge_w_out": edge_w_out, "edge_gain": edge_gain, "node_w_self": node_w_self, "node_w_agg": node_w_agg, "node_w_out": node_w_out, "node_gain": node_gain}


def layer_normalize(values):
    center = values - lax.optimization_barrier(jnp.mean(values, axis=-1, keepdims=True))
    spread = lax.optimization_barrier(jnp.mean(center * center, axis=-1, keepdims=True))
    return center * lax.rsqrt(spread + 1e-05)

def reference(node_feat, edge_feat, edge_slot, edge_recv, send_list, edge_w_edge, edge_w_send, edge_w_recv, edge_w_out, edge_gain, node_w_self, node_w_agg, node_w_out, node_gain):
    per_part = EDGE_DEV * N_EDGE
    partitions = jnp.arange(N_DOM, dtype=jnp.int32)
    slot_blocks = edge_slot.reshape(N_DOM, per_part)
    recv_blocks = edge_recv.reshape(N_DOM, per_part)
    feat_blocks = edge_feat.reshape(N_DOM, per_part, D)

    def one_partition(inputs):
        owner, slot_block, recv_block, feat_block = inputs
        beyond = jnp.maximum(slot_block - NODE_DEV, 0).astype(jnp.int32)
        source = (beyond // SLOT).astype(jnp.int32)
        position = (beyond % SLOT).astype(jnp.int32)
        listed = send_list[source, owner, position]
        sender = jnp.where(slot_block < NODE_DEV, owner * NODE_DEV + slot_block, source * NODE_DEV + listed).astype(jnp.int32)
        receiver = (owner * NODE_DEV + recv_block).astype(jnp.int32)
        edge_pre = jnp.dot(feat_block, edge_w_edge, preferred_element_type=jnp.float32)
        edge_pre = edge_pre + jnp.dot(node_feat[sender], edge_w_send, preferred_element_type=jnp.float32)
        edge_pre = edge_pre + jnp.dot(node_feat[receiver], edge_w_recv, preferred_element_type=jnp.float32)
        edge_hidden = jax.nn.silu(edge_pre).astype(jnp.bfloat16)
        message = layer_normalize(jnp.dot(edge_hidden, edge_w_out, preferred_element_type=jnp.float32)) * edge_gain
        new_edges = (feat_block.astype(jnp.float32) + message).astype(jnp.bfloat16)
        summed = jax.ops.segment_sum(message, recv_block, num_segments=NODE_DEV)
        return (new_edges, summed)
    new_edges, summed = lax.map(one_partition, (partitions, slot_blocks, recv_blocks, feat_blocks))
    aggregate_b = summed.reshape(NODES, D).astype(jnp.bfloat16)
    node_pre = jnp.dot(node_feat, node_w_self, preferred_element_type=jnp.float32)
    node_pre = node_pre + jnp.dot(aggregate_b, node_w_agg, preferred_element_type=jnp.float32)
    node_hidden = jax.nn.silu(node_pre).astype(jnp.bfloat16)
    node_update = layer_normalize(jnp.dot(node_hidden, node_w_out, preferred_element_type=jnp.float32)) * node_gain
    node_out = (node_feat.astype(jnp.float32) + node_update).astype(jnp.bfloat16)
    return (node_out, new_edges.reshape(EDGES, D))
```

```python
import functools

import jax
import jax.numpy as jnp
from jax import lax
from jax.experimental import pallas as pl
from jax.experimental.pallas import tpu as pltpu
from jax.sharding import PartitionSpec as P

F32 = jnp.float32
BF16 = jnp.bfloat16
LANE = 128
VMEM_BYTES = 40 * 1024 * 1024

W_EDGE, W_RECV, W_SEND, W_OUT, W_AGG, W_NODE = range(6)
HALF = 3


def whole(*shape):
    return pl.BlockSpec(shape, lambda i: (0,) * len(shape))


def one_of(index, *shape):
    return pl.BlockSpec((None,) + shape, lambda i: (index,) + (0,) * len(shape))


def call(body, outs, in_specs, flops, nbytes, scratch=(), out_specs=None):
    return pl.pallas_call(
        body,
        out_shape=outs,
        grid=(1,),
        in_specs=in_specs,
        out_specs=out_specs
        if out_specs is not None
        else jax.tree.map(lambda o: whole(*o.shape), outs),
        scratch_shapes=scratch,
        compiler_params=pltpu.CompilerParams(vmem_limit_bytes=VMEM_BYTES),
        cost_estimate=pl.CostEstimate(flops=flops, bytes_accessed=nbytes, transcendentals=0),
    )


def silu(v):
    return 0.5 * v * (1.0 + jnp.tanh(0.5 * v))


def normalize(v):
    center = v - jnp.mean(v, axis=-1, keepdims=True)
    spread = jnp.mean(center * center, axis=-1, keepdims=True)
    return center * lax.rsqrt(spread + 1e-05)


def dot(a, b):
    return jnp.dot(a, b, preferred_element_type=F32)


def shard_order():
    x = lax.axis_index("edge")
    core = lax.rem(lax.axis_index("dom"), 2)
    step = jnp.where(core == 0, 3, 1)
    return (x, lax.rem(x + step, 4), lax.rem(x + 4 - step, 4), lax.rem(x + 2, 4))


def columns(j):
    return pl.ds(pl.multiple_of(j * LANE, LANE), LANE)


def by_shard(ref, rows, order):
    return jnp.concatenate([ref[rows, columns(j)] for j in order], axis=1)


def stacked(refs):
    return jnp.concatenate([r[...] for r in refs], axis=0)


def column_of(row_block):
    return jnp.transpose(row_block.astype(F32))


def pack_kernel(*refs):
    shards, (packed, half, sem) = refs[:6], refs[6:]
    core = lax.rem(lax.axis_index("dom"), 2)
    copies = [pltpu.make_async_copy(s, packed.at[k], sem.at[k]) for k, s in enumerate(shards)]
    for c in copies:
        c.start()
    for side in range(2):
        @pl.when(core == side)
        def _():
            mine = [
                pltpu.make_async_copy(shards[HALF * side + k], half.at[k], sem.at[6 + k])
                for k in range(HALF)
            ]
            for c in mine:
                c.start()
            for c in mine:
                c.wait()
    for c in copies:
        c.wait()


def pick_kernel(listed_ref, node_ref, out_ref):
    slots, peers = listed_ref.shape
    nodes = node_ref.shape[0]
    mine = node_ref[:, columns(lax.axis_index("edge"))]
    listed = listed_ref[...].astype(F32).astype(BF16)
    rows = min(512, peers * slots)
    shift = slots.bit_length() - 1
    ones = jnp.ones((slots, nodes), BF16)
    for base in range(0, peers * slots, rows):
        place = base + lax.broadcasted_iota(jnp.int32, (rows, peers), 0)
        peer = lax.broadcasted_iota(jnp.int32, (rows, peers), 1)
        spread = jnp.where(lax.shift_right_logical(place, shift) == peer, 1.0, 0.0).astype(BF16)
        found = lax.dot_general(
            spread, listed, (((1,), (1,)), ((), ())), preferred_element_type=F32
        )
        slot = jnp.bitwise_and(lax.broadcasted_iota(jnp.int32, (rows, slots), 0), slots - 1)
        lane = lax.broadcasted_iota(jnp.int32, (rows, slots), 1)
        found = jnp.where(slot == lane, found, 0.0).astype(BF16)
        wanted = dot(found, ones)
        node = lax.broadcasted_iota(jnp.int32, (rows, nodes), 1).astype(F32)
        onehot = jnp.where(wanted == node, 1.0, 0.0).astype(BF16)
        out_ref[base : base + rows, :] = dot(onehot, mine).astype(BF16)


def choose_kernel(nodes, own_ref, left_ref, right_ref, far_ref, table_ref, out_ref):
    x = lax.axis_index("edge")
    entries = table_ref.shape[0]
    width = 256
    lane = lax.broadcasted_iota(jnp.int32, (LANE, width), 1).astype(F32)
    for ref, away in ((own_ref, 0), (left_ref, 3), (right_ref, 1), (far_ref, 2)):
        wanted = column_of(ref[...] - nodes)
        blocks = []
        for g in range(ref.shape[0]):
            total = jnp.zeros((LANE, LANE), F32)
            for base in range(0, entries, width):
                w = min(width, entries - base)
                onehot = jnp.where(
                    wanted[:, g : g + 1] - float(base) == lane[:, :w], 1.0, 0.0
                ).astype(BF16)
                total = total + dot(onehot, table_ref[base : base + w, :])
            blocks.append(total.astype(BF16))
        out_ref[lax.rem(x + away, 4), :, :] = jnp.concatenate(blocks, axis=1)


def base_kernel(
    edge_ref, node_ref, slot_ref, recv_ref,
    e0, e1, e2, e3, r0, r1, r2, r3, s0, s1, s2, s3, base_ref, table_ref,
):
    order = shard_order()
    nodes = node_ref.shape[0]
    by_node = by_shard(node_ref, slice(None), order)
    table_ref[0] = dot(by_node, stacked((s0, s1, s2, s3))).astype(BF16)
    table_ref[1] = dot(by_node, stacked((r0, r1, r2, r3))).astype(BF16)
    w_edge = stacked((e0, e1, e2, e3))
    slot = column_of(slot_ref[...])
    recv = column_of(recv_ref[...])
    lane = lax.broadcasted_iota(jnp.int32, (LANE, nodes), 1).astype(F32)
    for g in range(slot_ref.shape[0]):
        rows = slice(g * LANE, (g + 1) * LANE)
        from_slot = jnp.where(slot[:, g : g + 1] == lane, 1.0, 0.0).astype(BF16)
        from_recv = jnp.where(recv[:, g : g + 1] == lane, 1.0, 0.0).astype(BF16)
        total = dot(by_shard(edge_ref, rows, order), w_edge)
        total = total + dot(from_slot, table_ref[0])
        base_ref[rows, :] = total + dot(from_recv, table_ref[1])


def edge_kernel(
    edge_ref, base_ref, got_ref, recv_ref, node_ref, self_ref, gain_ref,
    s0, s1, s2, s3, o0, o1, o2, o3, a0, a1, a2, a3,
    out_ref, term_ref, hidden_ref, message_ref, total_ref,
):
    order = shard_order()
    w_send = stacked((s0, s1, s2, s3))
    w_out = stacked((o0, o1, o2, o3))
    edges, width = edge_ref.shape
    for g in range(edges // LANE):
        rows = slice(g * LANE, (g + 1) * LANE)
        sender = jnp.concatenate([got_ref[j, :, g * LANE : (g + 1) * LANE] for j in order], axis=1)
        hidden = silu(base_ref[rows, :] + dot(sender, w_send)).astype(BF16)
        hidden_ref[rows, :] = hidden
    for g in range(edges // LANE):
        rows = slice(g * LANE, (g + 1) * LANE)
        message = normalize(dot(by_shard(hidden_ref, rows, order), w_out)) * gain_ref[...]
        out_ref[rows, :] = (edge_ref[rows, :].astype(F32) + message).astype(BF16)
        message_ref[rows, :] = message.astype(BF16)
    nodes = node_ref.shape[0]
    node = lax.broadcasted_iota(jnp.int32, (nodes, LANE), 0)
    onehot = jnp.concatenate(
        [
            jnp.where(recv_ref[g : g + 1, :] == node, 1.0, 0.0).astype(BF16)
            for g in range(edges // LANE)
        ],
        axis=1,
    )
    total_ref[...] = dot(onehot, message_ref[...]).astype(BF16)
    term = dot(by_shard(total_ref, slice(None), order), stacked((a0, a1, a2, a3)))
    own = node_ref[:, columns(lax.axis_index("edge"))]
    term = (term + dot(own, self_ref[...])).astype(BF16)
    for j in range(term_ref.shape[0]):
        term_ref[j] = term


def node_kernel(terms_ref, node_ref, gain_ref, n0, n1, n2, n3, out_ref, hidden_ref):
    order = shard_order()
    terms = [terms_ref[j].astype(F32) for j in range(terms_ref.shape[0])]
    hidden_ref[...] = silu((terms[0] + terms[1]) + (terms[2] + terms[3])).astype(BF16)
    update = normalize(
        dot(by_shard(hidden_ref, slice(None), order), stacked((n0, n1, n2, n3)))
    )
    out_ref[...] = (node_ref[...].astype(F32) + update * gain_ref[...]).astype(BF16)


def local(
    node_feat, edge_feat, edge_slot, edge_recv, send_list, edge_w_edge, edge_w_send, edge_w_recv,
    edge_w_out, edge_gain, node_w_self, node_w_agg, node_w_out, node_gain,
):
    peers = lax.axis_size("dom")
    core = lax.rem(lax.axis_index("dom"), 2)
    nodes, width = node_feat.shape
    edges = edge_feat.shape[0]
    part, hid = edge_w_edge.shape
    slots = send_list.shape[2]
    entries = peers * slots
    groups = edges // LANE
    weight = jax.ShapeDtypeStruct

    def ring(away):
        return [(i, (i + away) % 4) for i in range(4)]

    both = [
        (d * 4 + i, d * 4 + (i + (1 if d % 2 == 0 else 3)) % 4)
        for d in range(peers)
        for i in range(4)
    ]
    swap = [(d, d ^ 1) for d in range(peers)]

    with jax.named_scope("pick_listed"):
        outgoing = call(
            pick_kernel,
            weight((entries, LANE), BF16),
            [whole(slots, peers), whole(nodes, width)],
            2 * entries * 640 * LANE,
            entries * 256 + nodes * width * 2,
        )(send_list[0].T, node_feat)
    with jax.named_scope("send_listed"):
        arrived = lax.all_to_all(
            outgoing.reshape(peers, slots, LANE), "dom", split_axis=0, concat_axis=0, tiled=True
        )
    with jax.named_scope("pack_shards"):
        anywhere = pl.BlockSpec(memory_space=pl.ANY)
        own_w, own_half = call(
            pack_kernel,
            (weight((6, part, hid), BF16), weight((HALF, part, hid), BF16)),
            [anywhere] * 6,
            0,
            18 * part * hid * 2,
            scratch=[pltpu.SemaphoreType.DMA((9,))],
            out_specs=(anywhere, anywhere),
        )(edge_w_edge, edge_w_recv, edge_w_send, edge_w_out, node_w_agg, node_w_out)
    with jax.named_scope("send_shards"):
        near_w = lax.ppermute(own_w, ("dom", "edge"), both)
        far_half = lax.ppermute(own_half, "edge", ring(2))
        across_w = lax.ppermute(near_w, "dom", swap)
        across_half = lax.ppermute(far_half, "dom", swap)
        low_half = lax.select(core == 0, far_half, across_half)
        high_half = lax.select(core == 0, across_half, far_half)
    with jax.named_scope("send_slots"):
        own_slot = edge_slot.reshape(groups, LANE)
        left_slot = lax.ppermute(own_slot, "edge", ring(1))
        right_slot = lax.ppermute(own_slot, "edge", ring(3))
        far_slot = lax.ppermute(own_slot, "edge", ring(2))
    recv = edge_recv.reshape(groups, LANE)

    def weights(k):
        far = low_half if k < HALF else high_half
        specs = [one_of(k, part, hid)] * 3 + [one_of(k % HALF, part, hid)]
        return (own_w, near_w, across_w, far), specs

    with jax.named_scope("edge_pre_local"):
        args, specs = zip(*[weights(k) for k in (W_EDGE, W_RECV, W_SEND)])
        base = call(
            base_kernel,
            weight((edges, hid), F32),
            [whole(edges, width), whole(nodes, width), whole(groups, LANE), whole(groups, LANE)]
            + sum(specs, []),
            2 * (2 * edges + 2 * nodes) * width * hid,
            edges * width * 6 + 3 * width * hid * 2,
            scratch=[pltpu.VMEM((2, nodes, hid), BF16)],
        )(edge_feat, node_feat, own_slot, recv, *sum(args, ()))
    with jax.named_scope("choose_senders"):
        chosen = call(
            functools.partial(choose_kernel, nodes),
            weight((4, LANE, groups * LANE), BF16),
            [whole(groups, LANE)] * 4 + [whole(entries, LANE)],
            2 * 4 * edges * entries * LANE,
            entries * LANE * 2 + 4 * edges * LANE * 2,
        )(own_slot, left_slot, right_slot, far_slot, arrived.reshape(entries, LANE))
    with jax.named_scope("send_senders"):
        got = lax.all_to_all(chosen, "edge", split_axis=0, concat_axis=0, tiled=True)
    with jax.named_scope("edge_update"):
        args, specs = zip(*[weights(k) for k in (W_SEND, W_OUT, W_AGG)])
        edge_out, term = call(
            edge_kernel,
            (weight((edges, width), BF16), weight((4, nodes, hid), BF16)),
            [
                whole(edges, width), whole(edges, hid), whole(4, LANE, groups * LANE),
                whole(groups, LANE), whole(nodes, width), whole(part, hid), whole(1, width),
            ]
            + sum(specs, []),
            2 * (2 * edges + 2 * nodes) * width * hid,
            edges * width * 10 + 3 * width * hid * 2,
            scratch=[
                pltpu.VMEM((edges, hid), BF16),
                pltpu.VMEM((edges, width), BF16),
                pltpu.VMEM((nodes, width), BF16),
            ],
        )(
            edge_feat, base, got, recv, node_feat, node_w_self, edge_gain.reshape(1, width),
            *sum(args, ()),
        )
    with jax.named_scope("send_terms"):
        terms = lax.all_to_all(term, "edge", split_axis=0, concat_axis=0, tiled=True)
    with jax.named_scope("node_update"):
        args, specs = weights(W_NODE)
        node_out = call(
            node_kernel,
            weight((nodes, width), BF16),
            [whole(4, nodes, hid), whole(nodes, width), whole(1, width)] + specs,
            2 * nodes * width * hid,
            nodes * width * 12 + width * hid * 2,
            scratch=[pltpu.VMEM((nodes, hid), BF16)],
        )(terms, node_feat, node_gain.reshape(1, width), *args)
    return (node_out, edge_out)


def solution(mesh):
    in_specs = (
        P("dom", None),
        P(("dom", "edge"), None),
        P(("dom", "edge")),
        P(("dom", "edge")),
        P("dom", None, None),
        P("edge", None),
        P("edge", None),
        P("edge", None),
        P("edge", None),
        P(),
        P("edge", None),
        P("edge", None),
        P("edge", None),
        P(),
    )
    out_specs = (P("dom", None), P(("dom", "edge"), None))
    return jax.shard_map(local, mesh=mesh, in_specs=in_specs, out_specs=out_specs, check_vma=False)
```

```python
import functools

import jax
import jax.numpy as jnp
from jax import lax
from jax.experimental import pallas as pl
from jax.experimental.pallas import tpu as pltpu
from jax.sharding import PartitionSpec as P

F32 = jnp.float32
BF16 = jnp.bfloat16
LANE = 128
VMEM_BYTES = 24 * 1024 * 1024

W_NODE, W_EDGE, W_RECV, W_SEND, W_OUT, W_AGG = range(6)
HALF = 3
NOTE = 16


def whole(*shape):
    return pl.BlockSpec(shape, lambda i: (0,) * len(shape))


def block_of(index, *shape):
    return pl.BlockSpec(shape, lambda i: (index,) + (0,) * (len(shape) - 1))


def in_hbm(*arrays):
    return [pltpu.with_memory_space_constraint(a, pltpu.HBM) for a in arrays]


def call(body, outs, in_specs, flops, nbytes, scratch=(), out_specs=None):
    return pl.pallas_call(
        body,
        out_shape=outs,
        grid=(1,),
        in_specs=in_specs,
        out_specs=out_specs
        if out_specs is not None
        else jax.tree.map(lambda o: whole(*o.shape), outs),
        scratch_shapes=scratch,
        compiler_params=pltpu.CompilerParams(vmem_limit_bytes=VMEM_BYTES),
        cost_estimate=pl.CostEstimate(flops=flops, bytes_accessed=nbytes, transcendentals=0),
    )


def silu(v):
    return 0.5 * v * (1.0 + jnp.tanh(0.5 * v))


def normalize(v):
    center = v - jnp.mean(v, axis=-1, keepdims=True)
    spread = jnp.mean(center * center, axis=-1, keepdims=True)
    return center * lax.rsqrt(spread + 1e-05)


def dot(a, b):
    return jnp.dot(a, b, preferred_element_type=F32)


def shard_order():
    x = lax.axis_index("edge")
    core = lax.rem(lax.axis_index("dom"), 2)
    step = jnp.where(core == 0, 3, 1)
    return (x, lax.rem(x + step, 4), lax.rem(x + 4 - step, 4), lax.rem(x + 2, 4))


def columns(j):
    return pl.ds(pl.multiple_of(j * LANE, LANE), LANE)


def by_shard(ref, rows, order):
    return jnp.concatenate([ref[rows, columns(j)] for j in order], axis=1)


def stacked(refs, place=0):
    return jnp.concatenate([r[place * LANE : (place + 1) * LANE, :] for r in refs], axis=0)


def column_of(row_block):
    return jnp.transpose(row_block.astype(F32))


def pick_kernel(listed_hbm, node_hbm, slot_hbm, *refs):
    shards = refs[:6]
    out_ref, packed, listed_ref, node_ref, slot_ref, note_ref, sem = refs[6:]
    part = shards[0].shape[0]
    mine = columns(lax.axis_index("edge"))
    first = [
        pltpu.make_async_copy(listed_hbm, listed_ref, sem.at[0]),
        pltpu.make_async_copy(node_hbm.at[:, mine], node_ref, sem.at[1]),
        pltpu.make_async_copy(slot_hbm, slot_ref, sem.at[2]),
    ]
    copies = []
    for k, shard in enumerate(shards):
        at = k * part + (NOTE if k >= HALF else 0)
        copies.append(pltpu.make_async_copy(shard, packed.at[at : at + part, :], sem.at[3 + k]))
    for c in first + copies:
        c.start()
    first[2].wait()
    groups = slot_ref.shape[0]
    note_ref[...] = jnp.zeros_like(note_ref)
    high = lax.shift_right_logical(slot_ref[...], 4)
    low = jnp.bitwise_and(slot_ref[...], 15)
    note_ref[0:NOTE, 0 : 2 * LANE] = jnp.concatenate(
        [
            jnp.concatenate([v.astype(F32), jnp.zeros((NOTE - groups, LANE), F32)], axis=0)
            for v in (high, low)
        ],
        axis=1,
    ).astype(BF16)
    for k, at in enumerate((HALF * part, 2 * HALF * part + NOTE)):
        copies.append(
            pltpu.make_async_copy(note_ref, packed.at[at : at + NOTE, :], sem.at[9 + k])
        )
        copies[-1].start()
    slots, peers = listed_ref.shape
    nodes = node_ref.shape[0]
    first[0].wait()
    listed = listed_ref[...].astype(F32).astype(BF16)
    first[1].wait()
    mine = node_ref[...]
    rows = min(512, peers * slots)
    shift = slots.bit_length() - 1
    ones = jnp.ones((slots, nodes), BF16)
    for base in range(0, peers * slots, rows):
        place = base + lax.broadcasted_iota(jnp.int32, (rows, peers), 0)
        peer = lax.broadcasted_iota(jnp.int32, (rows, peers), 1)
        spread = jnp.where(lax.shift_right_logical(place, shift) == peer, 1.0, 0.0).astype(BF16)
        found = lax.dot_general(
            spread, listed, (((1,), (1,)), ((), ())), preferred_element_type=F32
        )
        slot = jnp.bitwise_and(lax.broadcasted_iota(jnp.int32, (rows, slots), 0), slots - 1)
        lane = lax.broadcasted_iota(jnp.int32, (rows, slots), 1)
        found = jnp.where(slot == lane, found, 0.0).astype(BF16)
        wanted = dot(found, ones)
        node = lax.broadcasted_iota(jnp.int32, (rows, nodes), 1).astype(F32)
        onehot = jnp.where(wanted == node, 1.0, 0.0).astype(BF16)
        out_ref[base : base + rows, :] = dot(onehot, mine).astype(BF16)
    for c in copies:
        c.wait()


def noted(block, groups):
    v = block[:, 0 : 2 * LANE].astype(F32)
    return (v[:groups, :LANE] * 16.0 + v[:groups, LANE:]).astype(jnp.int32)


def choose_kernel(
    nodes, own_ref, across_ref, near_ref, low_ref, high_ref, table_ref, out_ref, block_ref, sem
):
    order = shard_order()
    groups = own_ref.shape[0]
    core = lax.rem(lax.axis_index("dom"), 2)
    far = jnp.where(core == 0, high_ref[...].astype(F32), low_ref[...].astype(F32))
    all_slots = (
        own_ref[...],
        noted(near_ref[...], groups),
        across_ref[...],
        noted(far, groups),
    )
    entries = table_ref.shape[0]
    width = 256
    lane = lax.broadcasted_iota(jnp.int32, (LANE, width), 1).astype(F32)
    copies = []
    for k, slots in enumerate(all_slots):
        wanted = column_of(slots - nodes)
        for g in range(groups):
            total = jnp.zeros((LANE, LANE), F32)
            for base in range(0, entries, width):
                w = min(width, entries - base)
                onehot = jnp.where(
                    wanted[:, g : g + 1] - float(base) == lane[:, :w], 1.0, 0.0
                ).astype(BF16)
                total = total + dot(onehot, table_ref[base : base + w, :])
            block_ref[k, :, g * LANE : (g + 1) * LANE] = total.astype(BF16)
        copies.append(pltpu.make_async_copy(block_ref.at[k], out_ref.at[order[k]], sem.at[k]))
        copies[-1].start()
    for c in copies:
        c.wait()


def base_kernel(
    edge_ref, node_ref, slot_ref, recv_ref,
    e0, e1, e2, e3, r0, r1, r2, r3, h0, h1, h2, h3, out_ref, table_ref, base_ref, sem,
):
    order = shard_order()
    nodes = node_ref.shape[0]
    by_node = by_shard(node_ref, slice(None), order)
    table_ref[0] = dot(by_node, stacked((h0, h1, h2, h3))).astype(BF16)
    table_ref[1] = dot(by_node, stacked((r0, r1, r2, r3))).astype(BF16)
    w_edge = stacked((e0, e1, e2, e3))
    slot = column_of(slot_ref[...])
    recv = column_of(recv_ref[...])
    lane = lax.broadcasted_iota(jnp.int32, (LANE, nodes), 1).astype(F32)
    copies = []
    for g in range(slot_ref.shape[0]):
        rows = slice(g * LANE, (g + 1) * LANE)
        from_slot = jnp.where(slot[:, g : g + 1] == lane, 1.0, 0.0).astype(BF16)
        from_recv = jnp.where(recv[:, g : g + 1] == lane, 1.0, 0.0).astype(BF16)
        total = dot(by_shard(edge_ref, rows, order), w_edge)
        total = total + dot(from_slot, table_ref[0])
        base_ref[rows, :] = total + dot(from_recv, table_ref[1])
        copies.append(pltpu.make_async_copy(base_ref.at[rows, :], out_ref.at[rows, :], sem.at[g]))
        copies[-1].start()
    for c in copies:
        c.wait()


def edge_kernel(
    edge_hbm, base_hbm, node_hbm, self_hbm, gain_hbm, got_ref, recv_ref, h0, h1, h2, h3,
    out_hbm, term_ref, edge_ref, base_ref, node_ref, self_ref, gain_ref, out_ref,
    hidden_ref, message_ref, total_ref, sem,
):
    order = shard_order()
    edges, width = edge_ref.shape
    mine = columns(lax.axis_index("edge"))
    blocks = [slice(g * LANE, (g + 1) * LANE) for g in range(edges // LANE)]
    base_in = [
        pltpu.make_async_copy(base_hbm.at[rows, :], base_ref.at[rows, :], sem.at[g])
        for g, rows in enumerate(blocks)
    ]
    later_in = [
        pltpu.make_async_copy(gain_hbm, gain_ref, sem.at[4]),
        pltpu.make_async_copy(edge_hbm, edge_ref, sem.at[5]),
        pltpu.make_async_copy(node_hbm.at[:, mine], node_ref, sem.at[6]),
        pltpu.make_async_copy(self_hbm, self_ref, sem.at[7]),
    ]
    for c in base_in + later_in:
        c.start()
    shards = (h0, h1, h2, h3)
    w_send = stacked(shards, 0)
    w_out = stacked(shards, 1)
    for g, rows in enumerate(blocks):
        sender = jnp.concatenate([got_ref[j, :, rows] for j in order], axis=1)
        before = dot(sender, w_send)
        base_in[g].wait()
        hidden_ref[rows, :] = silu(base_ref[rows, :] + before).astype(BF16)
    for c in later_in:
        c.wait()
    copies = []
    for g, rows in enumerate(blocks):
        message = normalize(dot(by_shard(hidden_ref, rows, order), w_out)) * gain_ref[...]
        out_ref[rows, :] = (edge_ref[rows, :].astype(F32) + message).astype(BF16)
        copies.append(pltpu.make_async_copy(out_ref.at[rows, :], out_hbm.at[rows, :], sem.at[8 + g]))
        copies[-1].start()
        message_ref[rows, :] = message.astype(BF16)
    node = lax.broadcasted_iota(jnp.int32, (node_ref.shape[0], LANE), 0)
    onehot = jnp.concatenate(
        [
            jnp.where(recv_ref[g : g + 1, :] == node, 1.0, 0.0).astype(BF16)
            for g in range(len(blocks))
        ],
        axis=1,
    )
    total_ref[...] = dot(onehot, message_ref[...]).astype(BF16)
    term = dot(by_shard(total_ref, slice(None), order), stacked(shards, 2))
    term = (term + dot(node_ref[...], self_ref[...])).astype(BF16)
    for j in range(term_ref.shape[0]):
        term_ref[j] = term
    for c in copies:
        c.wait()


def node_kernel(terms_ref, node_ref, gain_ref, n0, n1, n2, n3, out_ref, hidden_ref):
    order = shard_order()
    terms = [terms_ref[j].astype(F32) for j in range(terms_ref.shape[0])]
    hidden_ref[...] = silu((terms[0] + terms[1]) + (terms[2] + terms[3])).astype(BF16)
    update = normalize(
        dot(by_shard(hidden_ref, slice(None), order), stacked((n0, n1, n2, n3)))
    )
    out_ref[...] = (node_ref[...].astype(F32) + update * gain_ref[...]).astype(BF16)


def local(
    node_feat, edge_feat, edge_slot, edge_recv, send_list, edge_w_edge, edge_w_send, edge_w_recv,
    edge_w_out, edge_gain, node_w_self, node_w_agg, node_w_out, node_gain,
):
    peers = lax.axis_size("dom")
    core = lax.rem(lax.axis_index("dom"), 2)
    nodes, width = node_feat.shape
    edges = edge_feat.shape[0]
    part, hid = edge_w_edge.shape
    slots = send_list.shape[2]
    entries = peers * slots
    groups = edges // LANE
    weight = jax.ShapeDtypeStruct

    both = [
        (d * 4 + i, d * 4 + (i + (1 if d % 2 == 0 else 3)) % 4)
        for d in range(peers)
        for i in range(4)
    ]
    back = [(i, j) for j, i in both]
    swap = [(d, d ^ 1) for d in range(peers)]

    anywhere = pl.BlockSpec(memory_space=pltpu.HBM)
    dma = pltpu.SemaphoreType.DMA
    own_slot = edge_slot.reshape(groups, LANE)
    recv = edge_recv.reshape(groups, LANE)
    packed_rows = 2 * (HALF * part + NOTE)
    half_rows = HALF * part + NOTE

    with jax.named_scope("pick_listed"):
        outgoing, own_w = call(
            pick_kernel,
            (weight((entries, LANE), BF16), weight((packed_rows, hid), BF16)),
            [anywhere] * 9,
            2 * entries * 640 * LANE,
            entries * 256 + nodes * width * 2,
            scratch=[
                pltpu.VMEM((slots, peers), jnp.int32),
                pltpu.VMEM((nodes, LANE), BF16),
                pltpu.VMEM((groups, LANE), jnp.int32),
                pltpu.VMEM((NOTE, hid), BF16),
                dma((11,)),
            ],
            out_specs=(whole(entries, LANE), anywhere),
        )(
            *in_hbm(
                send_list[0].T, node_feat, own_slot,
                node_w_out, edge_w_edge, edge_w_recv, edge_w_send, edge_w_out, node_w_agg,
            )
        )
    with jax.named_scope("send_near"):
        near_w = lax.ppermute(own_w, ("dom", "edge"), both)
    with jax.named_scope("send_listed"):
        arrived = lax.all_to_all(
            outgoing.reshape(peers, slots, LANE), "dom", split_axis=0, concat_axis=0, tiled=True
        )
    with jax.named_scope("send_slots"):
        back_slot, _ = lax.optimization_barrier((own_slot, own_w))
        across_slot = lax.ppermute(back_slot, ("dom", "edge"), back)
    with jax.named_scope("send_far"):
        half = lax.dynamic_slice_in_dim(near_w, HALF * part * core, half_rows, 0)
        far_half = lax.ppermute(half, ("dom", "edge"), both)
    with jax.named_scope("swap_near"):
        across_w = lax.ppermute(near_w, "dom", swap)
    with jax.named_scope("swap_far"):
        across_half = lax.ppermute(far_half, "dom", swap)
        low_half = lax.select(core == 0, far_half[: half_rows - NOTE], across_half[: half_rows - NOTE])
        high_half = lax.select(core == 0, across_half[NOTE:], far_half[NOTE:])

    with jax.named_scope("choose_senders"):
        chosen = call(
            functools.partial(choose_kernel, nodes),
            weight((4, LANE, groups * LANE), BF16),
            [
                whole(groups, LANE), whole(groups, LANE),
                block_of(HALF * part // NOTE, NOTE, hid),
                block_of(0, NOTE, hid), block_of(HALF * part // NOTE, NOTE, hid),
                whole(entries, LANE),
            ],
            2 * 4 * edges * entries * LANE,
            entries * LANE * 2 + 4 * edges * LANE * 2,
            scratch=[pltpu.VMEM((4, LANE, groups * LANE), BF16), dma((4,))],
            out_specs=anywhere,
        )(
            own_slot, across_slot, near_w, far_half, far_half, arrived.reshape(entries, LANE),
        )
    with jax.named_scope("send_senders"):
        got = lax.all_to_all(chosen, "edge", split_axis=0, concat_axis=0, tiled=True)

    def low(k):
        return (own_w, near_w, across_w, low_half), [block_of(k, part, hid)] * 4

    high = (own_w, near_w, across_w, high_half)
    high_specs = [block_of(1, half_rows, hid)] * 3 + [whole(half_rows - NOTE, hid)]

    with jax.named_scope("edge_pre_local"):
        base = call(
            base_kernel,
            weight((edges, hid), F32),
            [whole(edges, width), whole(nodes, width), whole(groups, LANE), whole(groups, LANE)]
            + low(W_EDGE)[1] + low(W_RECV)[1] + high_specs,
            2 * (2 * edges + 2 * nodes) * width * hid,
            edges * width * 6 + 3 * width * hid * 2,
            scratch=[pltpu.VMEM((2, nodes, hid), BF16), pltpu.VMEM((edges, hid), F32), dma((groups,))],
            out_specs=anywhere,
        )(
            edge_feat, node_feat, own_slot, recv, *low(W_EDGE)[0], *low(W_RECV)[0], *high,
        )
    with jax.named_scope("edge_update"):
        edge_out, term = call(
            edge_kernel,
            (weight((edges, width), BF16), weight((4, nodes, hid), BF16)),
            [anywhere] * 5 + [whole(4, LANE, groups * LANE), whole(groups, LANE)] + high_specs,
            2 * (2 * edges + 2 * nodes) * width * hid,
            edges * width * 10 + 3 * width * hid * 2,
            scratch=[
                pltpu.VMEM((edges, width), BF16),
                pltpu.VMEM((edges, hid), F32),
                pltpu.VMEM((nodes, LANE), BF16),
                pltpu.VMEM((part, hid), BF16),
                pltpu.VMEM((1, width), F32),
                pltpu.VMEM((edges, width), BF16),
                pltpu.VMEM((edges, hid), BF16),
                pltpu.VMEM((edges, width), BF16),
                pltpu.VMEM((nodes, width), BF16),
                dma((12,)),
            ],
            out_specs=(anywhere, whole(4, nodes, hid)),
        )(
            *in_hbm(edge_feat, base, node_feat, node_w_self, edge_gain.reshape(1, width)),
            got, recv, *high,
        )
    with jax.named_scope("send_terms"):
        terms = lax.all_to_all(term, "edge", split_axis=0, concat_axis=0, tiled=True)
    with jax.named_scope("node_update"):
        args, specs = low(W_NODE)
        node_out = call(
            node_kernel,
            weight((nodes, width), BF16),
            [whole(4, nodes, hid), whole(nodes, width), whole(1, width)] + specs,
            2 * nodes * width * hid,
            nodes * width * 12 + width * hid * 2,
            scratch=[pltpu.VMEM((nodes, hid), BF16)],
        )(terms, node_feat, node_gain.reshape(1, width), *args)
    return (node_out, edge_out)


def solution(mesh):
    in_specs = (
        P("dom", None),
        P(("dom", "edge"), None),
        P(("dom", "edge")),
        P(("dom", "edge")),
        P("dom", None, None),
        P("edge", None),
        P("edge", None),
        P("edge", None),
        P("edge", None),
        P(),
        P("edge", None),
        P("edge", None),
        P("edge", None),
        P(),
    )
    out_specs = (P("dom", None), P(("dom", "edge"), None))
    return jax.shard_map(local, mesh=mesh, in_specs=in_specs, out_specs=out_specs, check_vma=False)
```

```python
import jax
import jax.numpy as jnp
from jax import lax
from jax.experimental import pallas as pl
from jax.experimental.pallas import tpu as pltpu
from jax.sharding import PartitionSpec as P

F32 = jnp.float32
BF16 = jnp.bfloat16
LANE = 128
VMEM_BYTES = 24 * 1024 * 1024

W_NODE, W_EDGE, W_RECV, W_SEND, W_OUT, W_AGG = range(6)
HALF = 3
NOTE = 16


def whole():
    return pl.BlockSpec(memory_space=pltpu.VMEM)


def in_hbm(*arrays):
    return [pltpu.with_memory_space_constraint(a, pltpu.HBM) for a in arrays]


def in_vmem(*arrays):
    return [pltpu.with_memory_space_constraint(a, pltpu.VMEM) for a in arrays]


def call(body, outs, in_specs, flops, nbytes, scratch=(), out_specs=None):
    return pl.pallas_call(
        body,
        out_shape=outs,
        in_specs=in_specs,
        out_specs=out_specs
        if out_specs is not None
        else jax.tree.map(lambda o: whole(), outs),
        scratch_shapes=scratch,
        compiler_params=pltpu.CompilerParams(vmem_limit_bytes=VMEM_BYTES),
        cost_estimate=pl.CostEstimate(flops=flops, bytes_accessed=nbytes, transcendentals=0),
    )


def silu(v):
    return 0.5 * v * (1.0 + jnp.tanh(0.5 * v))


def normalize(v):
    center = v - jnp.mean(v, axis=-1, keepdims=True)
    spread = jnp.mean(center * center, axis=-1, keepdims=True)
    return center * lax.rsqrt(spread + 1e-05)


def dot(a, b):
    return jnp.dot(a, b, preferred_element_type=F32)


def shard_order():
    x = lax.axis_index("edge")
    core = lax.rem(lax.axis_index("dom"), 2)
    step = jnp.where(core == 0, 3, 1)
    return (x, lax.rem(x + step, 4), lax.rem(x + 4 - step, 4), lax.rem(x + 2, 4))


def columns(j):
    return pl.ds(pl.multiple_of(j * LANE, LANE), LANE)


def by_shard(ref, rows, order):
    return jnp.concatenate([ref[rows, columns(j)] for j in order], axis=1)


def stacked(place, own_ref, near_ref, across_ref, far_ref, far_across_ref):
    at = place * LANE + (NOTE if place >= HALF else 0)
    parts = [r[at : at + LANE, :] for r in (own_ref, near_ref, across_ref)]
    high = place >= HALF
    at = (place % HALF) * LANE + (NOTE if high else 0)
    here = lax.rem(lax.axis_index("dom"), 2) == (1 if high else 0)
    rows = slice(at, at + LANE)
    parts.append(jnp.where(here, far_ref[rows, :], far_across_ref[rows, :]))
    return jnp.concatenate(parts, axis=0)


def column_of(row_block):
    return jnp.transpose(row_block.astype(F32))


def pick_kernel(listed_hbm, node_hbm, slot_hbm, *refs):
    shards = refs[:6]
    out_hbm, packed, listed_ref, node_ref, slot_ref, stage_ref, out_ref, sem = refs[6:]
    part, hid = shards[0].shape
    mine = columns(lax.axis_index("edge"))
    first = [
        pltpu.make_async_copy(listed_hbm, listed_ref, sem.at[0]),
        pltpu.make_async_copy(node_hbm.at[:, mine], node_ref, sem.at[1]),
        pltpu.make_async_copy(slot_hbm, slot_ref, sem.at[2]),
    ]
    copies = []
    for k, shard in enumerate(shards):
        at = k * part + (NOTE if k >= HALF else 0)
        copies.append(pltpu.make_async_copy(shard, packed.at[at : at + part, :], sem.at[3 + k]))
    for c in first + copies:
        c.start()
    slots, peers = listed_ref.shape
    nodes = node_ref.shape[0]
    node = lax.broadcasted_iota(jnp.int32, (1, nodes), 1).astype(F32)
    first[0].wait()
    listed = column_of(listed_ref[...])
    first[1].wait()
    chunk = min(32, peers)
    rows = chunk * slots
    for k, peer in enumerate(range(0, peers, chunk)):
        at = peer * slots
        onehot = jnp.concatenate(
            [
                jnp.where(
                    jnp.broadcast_to(listed[peer : peer + chunk, s : s + 1], (chunk, nodes)) == node,
                    1.0,
                    0.0,
                ).astype(BF16)
                for s in range(slots)
            ],
            axis=0,
        )
        found = dot(onehot, node_ref[...])
        for s in range(slots):
            stage_ref[pl.ds(at + s, chunk, stride=slots), :] = found[s * chunk : (s + 1) * chunk, :]
        out_ref[at : at + rows, :] = stage_ref[at : at + rows, :].astype(BF16)
        copies.append(
            pltpu.make_async_copy(
                out_ref.at[at : at + rows, :], out_hbm.at[at : at + rows, :], sem.at[9 + k]
            )
        )
        copies[-1].start()
    first[2].wait()
    groups = slot_ref.shape[0]
    high = lax.shift_right_logical(slot_ref[...], 4)
    low = jnp.bitwise_and(slot_ref[...], 15)
    note = jnp.concatenate(
        [v.astype(F32) for v in (high, low)] + [jnp.zeros((groups, hid - 2 * LANE), F32)], axis=1
    )
    note = jnp.concatenate([note, jnp.zeros((NOTE - groups, hid), F32)], axis=0).astype(BF16)
    for at in (HALF * part, 2 * HALF * part + NOTE):
        packed[at : at + NOTE, :] = note
    for c in copies:
        c.wait()


def noted(block, groups):
    v = block[:, 0 : 2 * LANE].astype(F32)
    return (v[:groups, :LANE] * 16.0 + v[:groups, LANE:]).astype(jnp.int32)


def choose_kernel(
    own_ref, across_ref, near_ref, far_ref, node_ref, table_hbm, out_ref, table_ref, sem
):
    nodes = node_ref.shape[0]
    half = (nodes + table_hbm.shape[0]) // 2
    split = max(half - nodes, 0)
    skip = nodes + split - half
    parts = [(table_hbm.at[split:, :], table_ref.at[skip:, LANE:])]
    if split:
        parts.append((table_hbm.at[:split, :], table_ref.at[nodes:, :LANE]))
    copies = [pltpu.make_async_copy(a, b, sem.at[k]) for k, (a, b) in enumerate(parts)]
    for c in copies:
        c.start()
    mine = node_ref[:, columns(lax.axis_index("edge"))]
    table_ref[: min(nodes, half), :LANE] = mine[: min(nodes, half), :]
    if skip:
        table_ref[:skip, LANE:] = mine[half:, :]
    order = shard_order()
    groups = own_ref.shape[0]
    core = lax.rem(lax.axis_index("dom"), 2)
    middle = slice(HALF * LANE, HALF * LANE + NOTE)
    far = jnp.where(core == 0, far_ref[middle, :].astype(F32), far_ref[0:NOTE, :].astype(F32))
    slots = jnp.concatenate(
        [own_ref[...], noted(near_ref[middle, :], groups), across_ref[...], noted(far, groups)],
        axis=0,
    )
    wanted = column_of(slots)
    second = wanted >= float(half)
    wanted = jnp.where(second, wanted - float(half), wanted)
    second = jnp.where(second, 1.0, 0.0)
    step = LANE if half % LANE == 0 else half
    for c in copies:
        c.wait()
    lane = lax.broadcasted_iota(jnp.int32, (1, step), 1).astype(F32)
    for k in range(4):
        for g in range(groups):
            at = k * groups + g
            place = jnp.broadcast_to(wanted[:, at : at + 1], (LANE, step))
            onehot = jnp.concatenate(
                [
                    jnp.where(place == lane + float(base), 1.0, 0.0).astype(BF16)
                    for base in range(0, half, step)
                ],
                axis=1,
            )
            found = dot(onehot, table_ref[...])
            later = jnp.broadcast_to(second[:, at : at + 1], (LANE, LANE)) > 0.5
            found = jnp.where(later, found[:, LANE:], found[:, :LANE])
            out_ref[order[k], :, g * LANE : (g + 1) * LANE] = found.astype(BF16)


def edge_kernel(
    edge_ref, node_ref, self_ref, gain_hbm, got_ref, recv_ref,
    own_w, near_w, across_w, far_w, far_across_w,
    out_ref, term_ref, hidden_ref, message_ref, total_ref, gain_ref, sem,
):
    gain_in = pltpu.make_async_copy(gain_hbm, gain_ref, sem)
    gain_in.start()
    order = shard_order()
    edges = edge_ref.shape[0]
    nodes = node_ref.shape[0]
    blocks = [slice(g * LANE, (g + 1) * LANE) for g in range(edges // LANE)]
    shards = (own_w, near_w, across_w, far_w, far_across_w)
    at_node = dot(by_shard(node_ref, slice(None), order), stacked(W_RECV, *shards)).astype(BF16)
    w_edge = stacked(W_EDGE, *shards)
    w_send = stacked(W_SEND, *shards)
    recv = column_of(recv_ref[...])
    lane = lax.broadcasted_iota(jnp.int32, (1, nodes), 1).astype(F32)
    for g, rows in enumerate(blocks):
        sender = jnp.concatenate([got_ref[j, :, rows] for j in order], axis=1)
        place = jnp.broadcast_to(recv[:, g : g + 1], (LANE, nodes))
        onehot = jnp.where(place == lane, 1.0, 0.0).astype(BF16)
        before = dot(by_shard(edge_ref, rows, order), w_edge) + dot(sender, w_send)
        hidden_ref[rows, :] = silu(before + dot(onehot, at_node)).astype(BF16)
    w_out = stacked(W_OUT, *shards)
    gain_in.wait()
    for rows in blocks:
        message = normalize(dot(by_shard(hidden_ref, rows, order), w_out)) * gain_ref[...]
        out_ref[rows, :] = (edge_ref[rows, :].astype(F32) + message).astype(BF16)
        message_ref[rows, :] = message.astype(BF16)
    node = lax.broadcasted_iota(jnp.int32, (nodes, LANE), 0)
    onehot = jnp.concatenate(
        [
            jnp.where(recv_ref[g : g + 1, :] == node, 1.0, 0.0).astype(BF16)
            for g in range(len(blocks))
        ],
        axis=1,
    )
    total_ref[...] = dot(onehot, message_ref[...]).astype(BF16)
    term = dot(by_shard(total_ref, slice(None), order), stacked(W_AGG, *shards))
    own = node_ref[:, columns(lax.axis_index("edge"))]
    term = (term + dot(own, self_ref[...])).astype(BF16)
    for j in range(term_ref.shape[0]):
        term_ref[j] = term


def node_kernel(
    terms_ref, node_ref, gain_ref, own_w, near_w, across_w, far_w, far_across_w,
    out_ref, hidden_ref,
):
    order = shard_order()
    terms = [terms_ref[j].astype(F32) for j in range(terms_ref.shape[0])]
    hidden_ref[...] = silu((terms[0] + terms[1]) + (terms[2] + terms[3])).astype(BF16)
    update = normalize(
        dot(
            by_shard(hidden_ref, slice(None), order),
            stacked(W_NODE, own_w, near_w, across_w, far_w, far_across_w),
        )
    )
    out_ref[...] = (node_ref[...].astype(F32) + update * gain_ref[...]).astype(BF16)


def local(
    node_feat, edge_feat, edge_slot, edge_recv, send_list, edge_w_edge, edge_w_send, edge_w_recv,
    edge_w_out, edge_gain, node_w_self, node_w_agg, node_w_out, node_gain,
):
    peers = lax.axis_size("dom")
    core = lax.rem(lax.axis_index("dom"), 2)
    nodes, width = node_feat.shape
    edges = edge_feat.shape[0]
    part, hid = edge_w_edge.shape
    slots = send_list.shape[2]
    entries = peers * slots
    groups = edges // LANE
    weight = jax.ShapeDtypeStruct

    both = [
        (d * 4 + i, d * 4 + (i + (1 if d % 2 == 0 else 3)) % 4)
        for d in range(peers)
        for i in range(4)
    ]
    back = [(i, j) for j, i in both]
    swap = [(d, d ^ 1) for d in range(peers)]

    anywhere = pl.BlockSpec(memory_space=pltpu.HBM)
    dma = pltpu.SemaphoreType.DMA
    own_slot = edge_slot.reshape(groups, LANE)
    recv = edge_recv.reshape(groups, LANE)
    packed_rows = 2 * (HALF * part + NOTE)
    half_rows = HALF * part + NOTE

    with jax.named_scope("pick_listed"):
        outgoing, own_w = call(
            pick_kernel,
            (pltpu.HBM((entries, LANE), BF16), weight((packed_rows, hid), BF16)),
            [anywhere] * 9,
            2 * entries * 640 * LANE,
            entries * 256 + nodes * width * 2,
            scratch=[
                pltpu.VMEM((slots, peers), jnp.int32),
                pltpu.VMEM((nodes, LANE), BF16),
                pltpu.VMEM((groups, LANE), jnp.int32),
                pltpu.VMEM((entries, LANE), F32),
                pltpu.VMEM((entries, LANE), BF16),
                dma((9 + max(1, peers // 32),)),
            ],
            out_specs=(anywhere, whole()),
        )(
            *in_hbm(
                send_list[0].T, node_feat, own_slot,
                node_w_out, edge_w_edge, edge_w_recv, edge_w_send, edge_w_out, node_w_agg,
            )
        )
    with jax.named_scope("send_near"):
        near_w = lax.ppermute(own_w, ("dom", "edge"), both)
    with jax.named_scope("send_listed"):
        arrived = lax.all_to_all(
            outgoing.reshape(peers, slots, LANE), "dom", split_axis=0, concat_axis=0, tiled=True
        )
    with jax.named_scope("send_slots"):
        half = lax.dynamic_slice_in_dim(near_w, HALF * part * core, half_rows, 0)
        half, back_slot = lax.optimization_barrier((half, own_slot))
        across_slot = lax.ppermute(back_slot, ("dom", "edge"), back)
    with jax.named_scope("send_far"):
        far_half = lax.ppermute(half, ("dom", "edge"), both)
    with jax.named_scope("swap_near"):
        near_again, across_slot = lax.optimization_barrier((near_w, across_slot))
        across_w = lax.ppermute(near_again, "dom", swap)
    with jax.named_scope("swap_far"):
        across_half = lax.ppermute(far_half, "dom", swap)
    shards = (own_w, near_w, across_w, far_half, across_half)

    with jax.named_scope("choose_senders"):
        chosen = call(
            choose_kernel,
            weight((4, LANE, groups * LANE), BF16),
            [whole()] * 5 + [anywhere],
            2 * 2 * edges * entries * LANE,
            entries * LANE * 2 + 4 * edges * LANE * 2,
            scratch=[pltpu.VMEM(((nodes + entries) // 2, 2 * LANE), BF16), dma((2,))],
        )(own_slot, across_slot, near_w, far_half, node_feat, arrived.reshape(entries, LANE))
    with jax.named_scope("send_senders"):
        got = lax.all_to_all(chosen, "edge", split_axis=0, concat_axis=0, tiled=True)
    with jax.named_scope("edge_update"):
        edge_out, term = call(
            edge_kernel,
            (weight((edges, width), BF16), weight((4, nodes, hid), BF16)),
            [whole()] * 3 + [anywhere] + [whole()] * 7,
            2 * (2 * edges + 2 * nodes) * width * hid,
            edges * width * 10 + 3 * width * hid * 2,
            scratch=[
                pltpu.VMEM((edges, hid), BF16),
                pltpu.VMEM((edges, width), BF16),
                pltpu.VMEM((nodes, width), BF16),
                pltpu.VMEM((1, width), F32),
                dma(()),
            ],
        )(
            *in_vmem(edge_feat, node_feat, node_w_self), *in_hbm(edge_gain.reshape(1, width)),
            got, *in_vmem(recv), *shards,
        )
    with jax.named_scope("send_terms"):
        terms = lax.all_to_all(term, "edge", split_axis=0, concat_axis=0, tiled=True)
    with jax.named_scope("node_update"):
        node_out = call(
            node_kernel,
            weight((nodes, width), BF16),
            [whole()] * 8,
            2 * nodes * width * hid,
            nodes * width * 12 + width * hid * 2,
            scratch=[pltpu.VMEM((nodes, hid), BF16)],
        )(terms, node_feat, node_gain.reshape(1, width), *shards)
    return (node_out, edge_out)


def solution(mesh):
    in_specs = (
        P("dom", None),
        P(("dom", "edge"), None),
        P(("dom", "edge")),
        P(("dom", "edge")),
        P("dom", None, None),
        P("edge", None),
        P("edge", None),
        P("edge", None),
        P("edge", None),
        P(),
        P("edge", None),
        P("edge", None),
        P("edge", None),
        P(),
    )
    out_specs = (P("dom", None), P(("dom", "edge"), None))
    return jax.shard_map(local, mesh=mesh, in_specs=in_specs, out_specs=out_specs, check_vma=False)
```

```python
import jax
import jax.numpy as jnp
from jax import lax
from jax.experimental import pallas as pl
from jax.experimental.pallas import tpu as pltpu
from jax.sharding import PartitionSpec as P

F32 = jnp.float32
BF16 = jnp.bfloat16
LANE = 128
VMEM_BYTES = 24 * 1024 * 1024

W_NODE, W_EDGE, W_RECV, W_SEND, W_OUT, W_AGG = range(6)
HALF = 3
NOTE = 16


def whole():
    return pl.BlockSpec(memory_space=pltpu.VMEM)


def in_hbm(*arrays):
    return [pltpu.with_memory_space_constraint(a, pltpu.HBM) for a in arrays]


def in_vmem(*arrays):
    return [pltpu.with_memory_space_constraint(a, pltpu.VMEM) for a in arrays]


def call(body, outs, in_specs, flops, nbytes, scratch=(), out_specs=None):
    return pl.pallas_call(
        body,
        out_shape=outs,
        in_specs=in_specs,
        out_specs=out_specs
        if out_specs is not None
        else jax.tree.map(lambda o: whole(), outs),
        scratch_shapes=scratch,
        compiler_params=pltpu.CompilerParams(vmem_limit_bytes=VMEM_BYTES),
        cost_estimate=pl.CostEstimate(flops=flops, bytes_accessed=nbytes, transcendentals=0),
    )


def silu(v):
    return 0.5 * v * (1.0 + jnp.tanh(0.5 * v))


def normalize(v):
    center = v - jnp.mean(v, axis=-1, keepdims=True)
    spread = jnp.mean(center * center, axis=-1, keepdims=True)
    return center * lax.rsqrt(spread + 1e-05)


def dot(a, b):
    return jnp.dot(a, b, preferred_element_type=F32)


def shard_order():
    x = lax.axis_index("edge")
    core = lax.rem(lax.axis_index("dom"), 2)
    step = jnp.where(core == 0, 3, 1)
    return (x, lax.rem(x + step, 4), lax.rem(x + 4 - step, 4), lax.rem(x + 2, 4))


def columns(j):
    return pl.ds(pl.multiple_of(j * LANE, LANE), LANE)


def by_shard(ref, rows, order):
    return jnp.concatenate([ref[rows, columns(j)] for j in order], axis=1)


def stacked(place, own_ref, near_ref, across_ref, far_ref, far_across_ref):
    at = place * LANE + (NOTE if place >= HALF else 0)
    parts = [r[at : at + LANE, :] for r in (own_ref, near_ref, across_ref)]
    high = place >= HALF
    at = (place % HALF) * LANE + (NOTE if high else 0)
    here = lax.rem(lax.axis_index("dom"), 2) == (1 if high else 0)
    rows = slice(at, at + LANE)
    parts.append(jnp.where(here, far_ref[rows, :], far_across_ref[rows, :]))
    return jnp.concatenate(parts, axis=0)


def column_of(row_block):
    return jnp.transpose(row_block.astype(F32))


def pick_kernel(listed_hbm, node_hbm, slot_hbm, *refs):
    shards = refs[:6]
    out_hbm, packed, listed_ref, node_ref, slot_ref, stage_ref, out_ref, sem = refs[6:]
    part, hid = shards[0].shape
    mine = columns(lax.axis_index("edge"))
    first = [
        pltpu.make_async_copy(listed_hbm, listed_ref, sem.at[0]),
        pltpu.make_async_copy(node_hbm.at[:, mine], node_ref, sem.at[1]),
        pltpu.make_async_copy(slot_hbm, slot_ref, sem.at[2]),
    ]
    copies = []
    for k, shard in enumerate(shards):
        at = k * part + (NOTE if k >= HALF else 0)
        copies.append(pltpu.make_async_copy(shard, packed.at[at : at + part, :], sem.at[3 + k]))
    for c in first + copies:
        c.start()
    slots, peers = listed_ref.shape
    nodes = node_ref.shape[0]
    node = lax.broadcasted_iota(jnp.int32, (1, nodes), 1).astype(F32)
    first[0].wait()
    listed = column_of(listed_ref[...])
    first[1].wait()
    chunk = min(32, peers)
    rows = chunk * slots
    for k, peer in enumerate(range(0, peers, chunk)):
        at = peer * slots
        onehot = jnp.concatenate(
            [
                jnp.where(
                    jnp.broadcast_to(listed[peer : peer + chunk, s : s + 1], (chunk, nodes)) == node,
                    1.0,
                    0.0,
                ).astype(BF16)
                for s in range(slots)
            ],
            axis=0,
        )
        found = dot(onehot, node_ref[...])
        for s in range(slots):
            stage_ref[pl.ds(at + s, chunk, stride=slots), :] = found[s * chunk : (s + 1) * chunk, :]
        out_ref[at : at + rows, :] = stage_ref[at : at + rows, :].astype(BF16)
        copies.append(
            pltpu.make_async_copy(
                out_ref.at[at : at + rows, :], out_hbm.at[at : at + rows, :], sem.at[9 + k]
            )
        )
        copies[-1].start()
    first[2].wait()
    groups = slot_ref.shape[0]
    high = lax.shift_right_logical(slot_ref[...], 4)
    low = jnp.bitwise_and(slot_ref[...], 15)
    note = jnp.concatenate(
        [v.astype(F32) for v in (high, low)] + [jnp.zeros((groups, hid - 2 * LANE), F32)], axis=1
    )
    note = jnp.concatenate([note, jnp.zeros((NOTE - groups, hid), F32)], axis=0).astype(BF16)
    for at in (HALF * part, 2 * HALF * part + NOTE):
        packed[at : at + NOTE, :] = note
    for c in copies:
        c.wait()


def noted(block, groups):
    v = block[:, 0 : 2 * LANE].astype(F32)
    return (v[:groups, :LANE] * 16.0 + v[:groups, LANE:]).astype(jnp.int32)


def choose_kernel(
    own_ref, across_ref, near_ref, far_ref, node_ref, table_hbm, recv_hbm, gain_hbm,
    out_ref, recv_ref, gain_ref, table_ref, sem,
):
    nodes = node_ref.shape[0]
    half = (nodes + table_hbm.shape[0]) // 2
    split = max(half - nodes, 0)
    skip = nodes + split - half
    parts = [(table_hbm.at[split:, :], table_ref.at[skip:, LANE:])]
    if split:
        parts.append((table_hbm.at[:split, :], table_ref.at[nodes:, :LANE]))
    copies = [pltpu.make_async_copy(a, b, sem.at[k]) for k, (a, b) in enumerate(parts)]
    ahead = [
        pltpu.make_async_copy(recv_hbm, recv_ref, sem.at[2]),
        pltpu.make_async_copy(gain_hbm, gain_ref, sem.at[3]),
    ]
    for c in copies + ahead:
        c.start()
    mine = node_ref[:, columns(lax.axis_index("edge"))]
    table_ref[: min(nodes, half), :LANE] = mine[: min(nodes, half), :]
    if skip:
        table_ref[:skip, LANE:] = mine[half:, :]
    order = shard_order()
    groups = own_ref.shape[0]
    core = lax.rem(lax.axis_index("dom"), 2)
    middle = slice(HALF * LANE, HALF * LANE + NOTE)
    far = jnp.where(core == 0, far_ref[middle, :].astype(F32), far_ref[0:NOTE, :].astype(F32))
    slots = jnp.concatenate(
        [own_ref[...], noted(near_ref[middle, :], groups), across_ref[...], noted(far, groups)],
        axis=0,
    )
    wanted = column_of(slots)
    second = wanted >= float(half)
    wanted = jnp.where(second, wanted - float(half), wanted)
    second = jnp.where(second, 1.0, 0.0)
    step = LANE if half % LANE == 0 else half
    lane = lax.broadcasted_iota(jnp.int32, (1, step), 1).astype(F32)

    def onehot_of(at):
        place = jnp.broadcast_to(wanted[:, at : at + 1], (LANE, step))
        return jnp.concatenate(
            [
                jnp.where(place == lane + float(base), 1.0, 0.0).astype(BF16)
                for base in range(0, half, step)
            ],
            axis=1,
        )

    early = [onehot_of(at) for at in range(groups)]
    for c in copies:
        c.wait()
    for k in range(4):
        for g in range(groups):
            at = k * groups + g
            found = dot(early[at] if at < groups else onehot_of(at), table_ref[...])
            later = jnp.broadcast_to(second[:, at : at + 1], (LANE, LANE)) > 0.5
            found = jnp.where(later, found[:, LANE:], found[:, :LANE])
            out_ref[order[k], :, g * LANE : (g + 1) * LANE] = found.astype(BF16)
    for c in ahead:
        c.wait()


def edge_kernel(
    edge_ref, node_ref, self_ref, gain_ref, got_ref, recv_ref,
    own_w, near_w, across_w, far_w, far_across_w,
    out_hbm, term_ref, hidden_ref, message_ref, total_ref, out_ref, sem,
):
    order = shard_order()
    edges = edge_ref.shape[0]
    nodes = node_ref.shape[0]
    blocks = [slice(g * LANE, (g + 1) * LANE) for g in range(edges // LANE)]
    shards = (own_w, near_w, across_w, far_w, far_across_w)
    at_node = dot(by_shard(node_ref, slice(None), order), stacked(W_RECV, *shards)).astype(BF16)
    w_edge = stacked(W_EDGE, *shards)
    w_send = stacked(W_SEND, *shards)
    recv = column_of(recv_ref[...])
    lane = lax.broadcasted_iota(jnp.int32, (1, nodes), 1).astype(F32)
    for g, rows in enumerate(blocks):
        sender = jnp.concatenate([got_ref[j, :, rows] for j in order], axis=1)
        place = jnp.broadcast_to(recv[:, g : g + 1], (LANE, nodes))
        onehot = jnp.where(place == lane, 1.0, 0.0).astype(BF16)
        before = dot(by_shard(edge_ref, rows, order), w_edge) + dot(sender, w_send)
        hidden_ref[rows, :] = silu(before + dot(onehot, at_node)).astype(BF16)
    w_out = stacked(W_OUT, *shards)
    copies = []
    for g, rows in enumerate(blocks):
        message = normalize(dot(by_shard(hidden_ref, rows, order), w_out)) * gain_ref[...]
        out_ref[rows, :] = (edge_ref[rows, :].astype(F32) + message).astype(BF16)
        copies.append(pltpu.make_async_copy(out_ref.at[rows, :], out_hbm.at[rows, :], sem.at[g]))
        copies[-1].start()
        message_ref[rows, :] = message.astype(BF16)
    node = lax.broadcasted_iota(jnp.int32, (nodes, LANE), 0)
    onehot = jnp.concatenate(
        [
            jnp.where(recv_ref[g : g + 1, :] == node, 1.0, 0.0).astype(BF16)
            for g in range(len(blocks))
        ],
        axis=1,
    )
    total_ref[...] = dot(onehot, message_ref[...]).astype(BF16)
    term = dot(by_shard(total_ref, slice(None), order), stacked(W_AGG, *shards))
    own = node_ref[:, columns(lax.axis_index("edge"))]
    term = (term + dot(own, self_ref[...])).astype(BF16)
    for j in range(term_ref.shape[0]):
        term_ref[j] = term
    for c in copies:
        c.wait()


def node_kernel(
    terms_ref, node_ref, gain_ref, own_w, near_w, across_w, far_w, far_across_w,
    out_hbm, hidden_ref, out_ref, sem,
):
    order = shard_order()
    w_node = stacked(W_NODE, own_w, near_w, across_w, far_w, far_across_w)
    copies = []
    for g in range(node_ref.shape[0] // LANE):
        rows = slice(g * LANE, (g + 1) * LANE)
        terms = [terms_ref[j, rows, :].astype(F32) for j in range(terms_ref.shape[0])]
        hidden = silu((terms[0] + terms[1]) + (terms[2] + terms[3]))
        hidden_ref[rows, :] = hidden.astype(BF16)
        update = normalize(dot(by_shard(hidden_ref, rows, order), w_node))
        out_ref[rows, :] = (node_ref[rows, :].astype(F32) + update * gain_ref[...]).astype(BF16)
        copies.append(pltpu.make_async_copy(out_ref.at[rows, :], out_hbm.at[rows, :], sem.at[g]))
        copies[-1].start()
    for c in copies:
        c.wait()


def local(
    node_feat, edge_feat, edge_slot, edge_recv, send_list, edge_w_edge, edge_w_send, edge_w_recv,
    edge_w_out, edge_gain, node_w_self, node_w_agg, node_w_out, node_gain,
):
    peers = lax.axis_size("dom")
    core = lax.rem(lax.axis_index("dom"), 2)
    nodes, width = node_feat.shape
    edges = edge_feat.shape[0]
    part, hid = edge_w_edge.shape
    slots = send_list.shape[2]
    entries = peers * slots
    groups = edges // LANE
    weight = jax.ShapeDtypeStruct

    both = [
        (d * 4 + i, d * 4 + (i + (1 if d % 2 == 0 else 3)) % 4)
        for d in range(peers)
        for i in range(4)
    ]
    back = [(i, j) for j, i in both]
    swap = [(d, d ^ 1) for d in range(peers)]

    anywhere = pl.BlockSpec(memory_space=pltpu.HBM)
    dma = pltpu.SemaphoreType.DMA
    own_slot = edge_slot.reshape(groups, LANE)
    recv = edge_recv.reshape(groups, LANE)
    packed_rows = 2 * (HALF * part + NOTE)
    half_rows = HALF * part + NOTE

    with jax.named_scope("pick_listed"):
        outgoing, own_w = call(
            pick_kernel,
            (pltpu.HBM((entries, LANE), BF16), weight((packed_rows, hid), BF16)),
            [anywhere] * 9,
            2 * entries * 640 * LANE,
            entries * 256 + nodes * width * 2,
            scratch=[
                pltpu.VMEM((slots, peers), jnp.int32),
                pltpu.VMEM((nodes, LANE), BF16),
                pltpu.VMEM((groups, LANE), jnp.int32),
                pltpu.VMEM((entries, LANE), F32),
                pltpu.VMEM((entries, LANE), BF16),
                dma((9 + max(1, peers // 32),)),
            ],
            out_specs=(anywhere, whole()),
        )(
            *in_hbm(
                send_list[0].T, node_feat, own_slot,
                node_w_out, edge_w_edge, edge_w_recv, edge_w_send, edge_w_out, node_w_agg,
            )
        )
    with jax.named_scope("send_near"):
        near_w = lax.ppermute(own_w, ("dom", "edge"), both)
    with jax.named_scope("send_listed"):
        arrived = lax.all_to_all(
            outgoing.reshape(peers, slots, LANE), "dom", split_axis=0, concat_axis=0, tiled=True
        )
    with jax.named_scope("send_slots"):
        half = lax.dynamic_slice_in_dim(near_w, HALF * part * core, half_rows, 0)
        half, back_slot = lax.optimization_barrier((half, own_slot))
        across_slot = lax.ppermute(back_slot, ("dom", "edge"), back)
    with jax.named_scope("send_far"):
        far_half = lax.ppermute(half, ("dom", "edge"), both)
    with jax.named_scope("swap_near"):
        near_again, across_slot = lax.optimization_barrier((near_w, across_slot))
        across_w = lax.ppermute(near_again, "dom", swap)
    with jax.named_scope("swap_far"):
        across_half = lax.ppermute(far_half, "dom", swap)
    shards = (own_w, near_w, across_w, far_half, across_half)

    with jax.named_scope("choose_senders"):
        chosen, recv_again, gain_again = call(
            choose_kernel,
            (
                weight((4, LANE, groups * LANE), BF16),
                pltpu.VMEM((groups, LANE), jnp.int32),
                pltpu.VMEM((1, width), F32),
            ),
            [whole()] * 5 + [anywhere] * 3,
            2 * 2 * edges * entries * LANE,
            entries * LANE * 2 + 4 * edges * LANE * 2,
            scratch=[pltpu.VMEM(((nodes + entries) // 2, 2 * LANE), BF16), dma((4,))],
            out_specs=(whole(),) * 3,
        )(
            own_slot, across_slot, near_w, far_half, node_feat, arrived.reshape(entries, LANE),
            *in_hbm(recv, edge_gain.reshape(1, width)),
        )
    with jax.named_scope("send_senders"):
        got = lax.all_to_all(chosen, "edge", split_axis=0, concat_axis=0, tiled=True)
    with jax.named_scope("edge_update"):
        edge_out, term = call(
            edge_kernel,
            (pltpu.HBM((edges, width), BF16), weight((4, nodes, hid), BF16)),
            [whole()] * 11,
            2 * (2 * edges + 2 * nodes) * width * hid,
            edges * width * 10 + 3 * width * hid * 2,
            scratch=[
                pltpu.VMEM((edges, hid), BF16),
                pltpu.VMEM((edges, width), BF16),
                pltpu.VMEM((nodes, width), BF16),
                pltpu.VMEM((edges, width), BF16),
                dma((groups,)),
            ],
            out_specs=(anywhere, whole()),
        )(
            *in_vmem(edge_feat, node_feat, node_w_self, gain_again),
            got, *in_vmem(recv_again), *shards,
        )
    with jax.named_scope("send_terms"):
        terms = lax.all_to_all(term, "edge", split_axis=0, concat_axis=0, tiled=True)
    with jax.named_scope("node_update"):
        node_out = call(
            node_kernel,
            pltpu.HBM((nodes, width), BF16),
            [whole()] * 8,
            2 * nodes * width * hid,
            nodes * width * 12 + width * hid * 2,
            scratch=[
                pltpu.VMEM((nodes, hid), BF16),
                pltpu.VMEM((nodes, width), BF16),
                dma((nodes // LANE,)),
            ],
            out_specs=anywhere,
        )(terms, node_feat, node_gain.reshape(1, width), *shards)
    return (node_out, edge_out)


def solution(mesh):
    in_specs = (
        P("dom", None),
        P(("dom", "edge"), None),
        P(("dom", "edge")),
        P(("dom", "edge")),
        P("dom", None, None),
        P("edge", None),
        P("edge", None),
        P("edge", None),
        P("edge", None),
        P(),
        P("edge", None),
        P("edge", None),
        P("edge", None),
        P(),
    )
    out_specs = (P("dom", None), P(("dom", "edge"), None))
    return jax.shard_map(local, mesh=mesh, in_specs=in_specs, out_specs=out_specs, check_vma=False)
```

```python
import jax
import jax.numpy as jnp
from jax import lax
from jax.experimental import pallas as pl
from jax.experimental.pallas import tpu as pltpu
from jax.sharding import PartitionSpec as P

F32 = jnp.float32
BF16 = jnp.bfloat16
LANE = 128
VMEM_BYTES = 24 * 1024 * 1024

W_NODE, W_EDGE, W_RECV, W_SEND, W_OUT, W_AGG = range(6)
HALF = 3
NOTE = 16


def whole():
    return pl.BlockSpec(memory_space=pltpu.VMEM)


def in_hbm(*arrays):
    return [pltpu.with_memory_space_constraint(a, pltpu.HBM) for a in arrays]


def in_vmem(*arrays):
    return [pltpu.with_memory_space_constraint(a, pltpu.VMEM) for a in arrays]


def call(body, outs, in_specs, flops, nbytes, scratch=(), out_specs=None):
    return pl.pallas_call(
        body,
        out_shape=outs,
        in_specs=in_specs,
        out_specs=out_specs
        if out_specs is not None
        else jax.tree.map(lambda o: whole(), outs),
        scratch_shapes=scratch,
        compiler_params=pltpu.CompilerParams(vmem_limit_bytes=VMEM_BYTES),
        cost_estimate=pl.CostEstimate(flops=flops, bytes_accessed=nbytes, transcendentals=0),
    )


def silu(v):
    return 0.5 * v * (1.0 + jnp.tanh(0.5 * v))


def normalize(v):
    center = v - jnp.mean(v, axis=-1, keepdims=True)
    spread = jnp.mean(center * center, axis=-1, keepdims=True)
    return center * lax.rsqrt(spread + 1e-05)


def dot(a, b):
    return jnp.dot(a, b, preferred_element_type=F32)


def shard_order():
    x = lax.axis_index("edge")
    core = lax.rem(lax.axis_index("dom"), 2)
    step = jnp.where(core == 0, 3, 1)
    return (x, lax.rem(x + step, 4), lax.rem(x + 4 - step, 4), lax.rem(x + 2, 4))


def columns(j):
    return pl.ds(pl.multiple_of(j * LANE, LANE), LANE)


def by_shard(ref, rows, order):
    return jnp.concatenate([ref[rows, columns(j)] for j in order], axis=1)


def stacked(place, own_ref, near_ref, across_ref, far_ref, far_across_ref):
    at = place * LANE + (NOTE if place >= HALF else 0)
    parts = [r[at : at + LANE, :] for r in (own_ref, near_ref, across_ref)]
    high = place >= HALF
    at = (place % HALF) * LANE + (NOTE if high else 0)
    here = lax.rem(lax.axis_index("dom"), 2) == (1 if high else 0)
    rows = slice(at, at + LANE)
    parts.append(jnp.where(here, far_ref[rows, :], far_across_ref[rows, :]))
    return jnp.concatenate(parts, axis=0)


def column_of(row_block):
    return jnp.transpose(row_block.astype(F32))


def pick_kernel(listed_hbm, node_hbm, slot_hbm, *refs):
    shards = refs[:6]
    out_hbm, packed, listed_ref, node_ref, slot_ref, stage_ref, out_ref, sem = refs[6:]
    part, hid = shards[0].shape
    mine = columns(lax.axis_index("edge"))
    first = [
        pltpu.make_async_copy(listed_hbm, listed_ref, sem.at[0]),
        pltpu.make_async_copy(node_hbm.at[:, mine], node_ref, sem.at[1]),
        pltpu.make_async_copy(slot_hbm, slot_ref, sem.at[2]),
    ]
    copies = []
    for k, shard in enumerate(shards):
        at = k * part + (NOTE if k >= HALF else 0)
        copies.append(pltpu.make_async_copy(shard, packed.at[at : at + part, :], sem.at[3 + k]))
    for c in first + copies:
        c.start()
    slots, peers = listed_ref.shape
    nodes = node_ref.shape[0]
    node = lax.broadcasted_iota(jnp.int32, (1, nodes), 1).astype(F32)
    first[0].wait()
    listed = column_of(listed_ref[...])
    first[1].wait()
    chunk = min(64, peers)
    rows = chunk * slots
    for k, peer in enumerate(range(0, peers, chunk)):
        at = peer * slots
        onehot = jnp.concatenate(
            [
                jnp.where(
                    jnp.broadcast_to(listed[peer : peer + chunk, s : s + 1], (chunk, nodes)) == node,
                    1.0,
                    0.0,
                ).astype(BF16)
                for s in range(slots)
            ],
            axis=0,
        )
        found = dot(onehot, node_ref[...])
        for s in range(slots):
            stage_ref[pl.ds(at + s, chunk, stride=slots), :] = found[s * chunk : (s + 1) * chunk, :]
        out_ref[at : at + rows, :] = stage_ref[at : at + rows, :].astype(BF16)
        copies.append(
            pltpu.make_async_copy(
                out_ref.at[at : at + rows, :], out_hbm.at[at : at + rows, :], sem.at[9 + k]
            )
        )
        copies[-1].start()
    first[2].wait()
    groups = slot_ref.shape[0]
    high = lax.shift_right_logical(slot_ref[...], 4)
    low = jnp.bitwise_and(slot_ref[...], 15)
    note = jnp.concatenate(
        [v.astype(F32) for v in (high, low)] + [jnp.zeros((groups, hid - 2 * LANE), F32)], axis=1
    )
    note = jnp.concatenate([note, jnp.zeros((NOTE - groups, hid), F32)], axis=0).astype(BF16)
    for at in (HALF * part, 2 * HALF * part + NOTE):
        packed[at : at + NOTE, :] = note
    for c in copies:
        c.wait()


def noted(block, groups):
    v = block[:, 0 : 2 * LANE].astype(F32)
    return (v[:groups, :LANE] * 16.0 + v[:groups, LANE:]).astype(jnp.int32)


def choose_kernel(
    own_ref, across_ref, near_ref, far_ref, node_ref, table_hbm, recv_hbm, gain_hbm,
    out_ref, recv_ref, gain_ref, table_ref, sem,
):
    nodes = node_ref.shape[0]
    half = (nodes + table_hbm.shape[0]) // 2
    split = max(half - nodes, 0)
    skip = nodes + split - half
    parts = [(table_hbm.at[split:, :], table_ref.at[skip:, LANE:])]
    if split:
        parts.append((table_hbm.at[:split, :], table_ref.at[nodes:, :LANE]))
    copies = [pltpu.make_async_copy(a, b, sem.at[k]) for k, (a, b) in enumerate(parts)]
    ahead = [
        pltpu.make_async_copy(recv_hbm, recv_ref, sem.at[2]),
        pltpu.make_async_copy(gain_hbm, gain_ref, sem.at[3]),
    ]
    for c in copies + ahead:
        c.start()
    mine = node_ref[:, columns(lax.axis_index("edge"))]
    table_ref[: min(nodes, half), :LANE] = mine[: min(nodes, half), :]
    if skip:
        table_ref[:skip, LANE:] = mine[half:, :]
    order = shard_order()
    groups = own_ref.shape[0]
    core = lax.rem(lax.axis_index("dom"), 2)
    middle = slice(HALF * LANE, HALF * LANE + NOTE)
    far = jnp.where(core == 0, far_ref[middle, :].astype(F32), far_ref[0:NOTE, :].astype(F32))
    slots = jnp.concatenate(
        [own_ref[...], noted(near_ref[middle, :], groups), across_ref[...], noted(far, groups)],
        axis=0,
    )
    wanted = column_of(slots)
    second = wanted >= float(half)
    wanted = jnp.where(second, wanted - float(half), wanted)
    second = jnp.where(second, 1.0, 0.0)
    step = LANE if half % LANE == 0 else half
    lane = lax.broadcasted_iota(jnp.int32, (1, step), 1).astype(F32)

    def onehot_of(at):
        place = jnp.broadcast_to(wanted[:, at : at + 1], (LANE, step))
        return jnp.concatenate(
            [
                jnp.where(place == lane + float(base), 1.0, 0.0).astype(BF16)
                for base in range(0, half, step)
            ],
            axis=1,
        )

    early = [onehot_of(at) for at in range(groups)]
    for c in copies:
        c.wait()
    for k in range(4):
        for g in range(groups):
            at = k * groups + g
            found = dot(early[at] if at < groups else onehot_of(at), table_ref[...])
            later = jnp.broadcast_to(second[:, at : at + 1], (LANE, LANE)) > 0.5
            found = jnp.where(later, found[:, LANE:], found[:, :LANE])
            out_ref[order[k], :, g * LANE : (g + 1) * LANE] = found.astype(BF16)
    for c in ahead:
        c.wait()


def edge_kernel(
    edge_ref, node_ref, self_ref, gain_ref, got_ref, recv_ref,
    own_w, near_w, across_w, far_w, far_across_w,
    out_hbm, term_ref, hidden_ref, message_ref, total_ref, out_ref, sem,
):
    order = shard_order()
    edges = edge_ref.shape[0]
    nodes = node_ref.shape[0]
    blocks = [slice(g * LANE, (g + 1) * LANE) for g in range(edges // LANE)]
    shards = (own_w, near_w, across_w, far_w, far_across_w)
    at_node = dot(by_shard(node_ref, slice(None), order), stacked(W_RECV, *shards)).astype(BF16)
    w_edge = stacked(W_EDGE, *shards)
    w_send = stacked(W_SEND, *shards)
    recv = column_of(recv_ref[...])
    lane = lax.broadcasted_iota(jnp.int32, (1, nodes), 1).astype(F32)
    for g, rows in enumerate(blocks):
        sender = jnp.concatenate([got_ref[j, :, rows] for j in order], axis=1)
        place = jnp.broadcast_to(recv[:, g : g + 1], (LANE, nodes))
        onehot = jnp.where(place == lane, 1.0, 0.0).astype(BF16)
        before = dot(by_shard(edge_ref, rows, order), w_edge) + dot(sender, w_send)
        hidden_ref[rows, :] = silu(before + dot(onehot, at_node)).astype(BF16)
    w_out = stacked(W_OUT, *shards)
    copies = []
    for g, rows in enumerate(blocks):
        message = normalize(dot(by_shard(hidden_ref, rows, order), w_out)) * gain_ref[...]
        out_ref[rows, :] = (edge_ref[rows, :].astype(F32) + message).astype(BF16)
        copies.append(pltpu.make_async_copy(out_ref.at[rows, :], out_hbm.at[rows, :], sem.at[g]))
        copies[-1].start()
        message_ref[rows, :] = message.astype(BF16)
    node = lax.broadcasted_iota(jnp.int32, (nodes, LANE), 0)
    onehot = jnp.concatenate(
        [
            jnp.where(recv_ref[g : g + 1, :] == node, 1.0, 0.0).astype(BF16)
            for g in range(len(blocks))
        ],
        axis=1,
    )
    total_ref[...] = dot(onehot, message_ref[...]).astype(BF16)
    term = dot(by_shard(total_ref, slice(None), order), stacked(W_AGG, *shards))
    own = node_ref[:, columns(lax.axis_index("edge"))]
    term = (term + dot(own, self_ref[...])).astype(BF16)
    for j in range(term_ref.shape[0]):
        term_ref[j] = term
    for c in copies:
        c.wait()


def node_kernel(
    terms_ref, node_ref, gain_ref, own_w, near_w, across_w, far_w, far_across_w,
    out_hbm, hidden_ref, out_ref, sem,
):
    order = shard_order()
    w_node = stacked(W_NODE, own_w, near_w, across_w, far_w, far_across_w)
    copies = []
    for g in range(node_ref.shape[0] // LANE):
        rows = slice(g * LANE, (g + 1) * LANE)
        terms = [terms_ref[j, rows, :].astype(F32) for j in range(terms_ref.shape[0])]
        hidden = silu((terms[0] + terms[1]) + (terms[2] + terms[3]))
        hidden_ref[rows, :] = hidden.astype(BF16)
        update = normalize(dot(by_shard(hidden_ref, rows, order), w_node))
        out_ref[rows, :] = (node_ref[rows, :].astype(F32) + update * gain_ref[...]).astype(BF16)
        copies.append(pltpu.make_async_copy(out_ref.at[rows, :], out_hbm.at[rows, :], sem.at[g]))
        copies[-1].start()
    for c in copies:
        c.wait()


def local(
    node_feat, edge_feat, edge_slot, edge_recv, send_list, edge_w_edge, edge_w_send, edge_w_recv,
    edge_w_out, edge_gain, node_w_self, node_w_agg, node_w_out, node_gain,
):
    peers = lax.axis_size("dom")
    core = lax.rem(lax.axis_index("dom"), 2)
    nodes, width = node_feat.shape
    edges = edge_feat.shape[0]
    part, hid = edge_w_edge.shape
    slots = send_list.shape[2]
    entries = peers * slots
    groups = edges // LANE
    weight = jax.ShapeDtypeStruct

    both = [
        (d * 4 + i, d * 4 + (i + (1 if d % 2 == 0 else 3)) % 4)
        for d in range(peers)
        for i in range(4)
    ]
    back = [(i, j) for j, i in both]
    swap = [(d, d ^ 1) for d in range(peers)]

    anywhere = pl.BlockSpec(memory_space=pltpu.HBM)
    dma = pltpu.SemaphoreType.DMA
    own_slot = edge_slot.reshape(groups, LANE)
    recv = edge_recv.reshape(groups, LANE)
    packed_rows = 2 * (HALF * part + NOTE)
    half_rows = HALF * part + NOTE

    with jax.named_scope("pick_listed"):
        outgoing, own_w = call(
            pick_kernel,
            (pltpu.HBM((entries, LANE), BF16), weight((packed_rows, hid), BF16)),
            [anywhere] * 9,
            2 * entries * 640 * LANE,
            entries * 256 + nodes * width * 2,
            scratch=[
                pltpu.VMEM((slots, peers), jnp.int32),
                pltpu.VMEM((nodes, LANE), BF16),
                pltpu.VMEM((groups, LANE), jnp.int32),
                pltpu.VMEM((entries + slots, LANE), F32),
                pltpu.VMEM((entries, LANE), BF16),
                dma((9 + max(1, peers // 32),)),
            ],
            out_specs=(anywhere, whole()),
        )(
            *in_hbm(
                send_list[0].T, node_feat, own_slot,
                node_w_out, edge_w_edge, edge_w_recv, edge_w_send, edge_w_out, node_w_agg,
            )
        )
    with jax.named_scope("send_near"):
        near_w = lax.ppermute(own_w, ("dom", "edge"), both)
    with jax.named_scope("send_listed"):
        arrived = lax.all_to_all(
            outgoing.reshape(peers, slots, LANE), "dom", split_axis=0, concat_axis=0, tiled=True
        )
    with jax.named_scope("send_slots"):
        half = lax.dynamic_slice_in_dim(near_w, HALF * part * core, half_rows, 0)
        half, back_slot = lax.optimization_barrier((half, own_slot))
        across_slot = lax.ppermute(back_slot, ("dom", "edge"), back)
    with jax.named_scope("send_far"):
        far_half = lax.ppermute(half, ("dom", "edge"), both)
    with jax.named_scope("swap_near"):
        near_again, across_slot = lax.optimization_barrier((near_w, across_slot))
        across_w = lax.ppermute(near_again, "dom", swap)
    with jax.named_scope("swap_far"):
        across_half = lax.ppermute(far_half, "dom", swap)
    shards = (own_w, near_w, across_w, far_half, across_half)

    with jax.named_scope("choose_senders"):
        chosen, recv_again, gain_again = call(
            choose_kernel,
            (
                weight((4, LANE, groups * LANE), BF16),
                pltpu.VMEM((groups, LANE), jnp.int32),
                pltpu.VMEM((1, width), F32),
            ),
            [whole()] * 5 + [anywhere] * 3,
            2 * 2 * edges * entries * LANE,
            entries * LANE * 2 + 4 * edges * LANE * 2,
            scratch=[pltpu.VMEM(((nodes + entries) // 2, 2 * LANE), BF16), dma((4,))],
            out_specs=(whole(),) * 3,
        )(
            own_slot, across_slot, near_w, far_half, node_feat, arrived.reshape(entries, LANE),
            *in_hbm(recv, edge_gain.reshape(1, width)),
        )
    with jax.named_scope("send_senders"):
        got = lax.all_to_all(chosen, "edge", split_axis=0, concat_axis=0, tiled=True)
    with jax.named_scope("edge_update"):
        edge_out, term = call(
            edge_kernel,
            (pltpu.HBM((edges, width), BF16), weight((4, nodes, hid), BF16)),
            [whole()] * 11,
            2 * (2 * edges + 2 * nodes) * width * hid,
            edges * width * 10 + 3 * width * hid * 2,
            scratch=[
                pltpu.VMEM((edges, hid), BF16),
                pltpu.VMEM((edges, width), BF16),
                pltpu.VMEM((nodes, width), BF16),
                pltpu.VMEM((edges, width), BF16),
                dma((groups,)),
            ],
            out_specs=(anywhere, whole()),
        )(
            *in_vmem(edge_feat, node_feat, node_w_self, gain_again),
            got, *in_vmem(recv_again), *shards,
        )
    with jax.named_scope("send_terms"):
        terms = lax.all_to_all(term, "edge", split_axis=0, concat_axis=0, tiled=True)
    with jax.named_scope("node_update"):
        node_out = call(
            node_kernel,
            pltpu.HBM((nodes, width), BF16),
            [whole()] * 8,
            2 * nodes * width * hid,
            nodes * width * 12 + width * hid * 2,
            scratch=[
                pltpu.VMEM((nodes, hid), BF16),
                pltpu.VMEM((nodes, width), BF16),
                dma((nodes // LANE,)),
            ],
            out_specs=anywhere,
        )(terms, node_feat, node_gain.reshape(1, width), *shards)
    return (node_out, edge_out)


def solution(mesh):
    in_specs = (
        P("dom", None),
        P(("dom", "edge"), None),
        P(("dom", "edge")),
        P(("dom", "edge")),
        P("dom", None, None),
        P("edge", None),
        P("edge", None),
        P("edge", None),
        P("edge", None),
        P(),
        P("edge", None),
        P("edge", None),
        P("edge", None),
        P(),
    )
    out_specs = (P("dom", None), P(("dom", "edge"), None))
    return jax.shard_map(local, mesh=mesh, in_specs=in_specs, out_specs=out_specs, check_vma=False)
```
